32 devices in a mesh: group: 2 (over x), lev: 2 (over core), row: 8 (over z, y).
Axes of the slice: x: 2, y: 2, z: 4, core: 2. Of those that a mesh axis runs over, the one named last changes fastest.
Arguments:
- fields: bfloat16 [6, 90, 64, 1024], P('group', 'lev', 'row'), parts along dimension 0, may hold values from -6 to 6
- vertical_modes: bfloat16 [8, 90, 64, 1024], P(None, 'lev', 'row'), may hold values from -0.625 to 0.625
- diffusivity: float32 [64, 1024], P('row'), may hold values from 0.05 to 0.245
- land_mask: int32 [64, 1024], P('row'), may hold values 0 or 1
- wet_levels: int32 [64, 1024], P('row'), may hold values from 1 to 90
Outputs:
- filtered: bfloat16 [6, 90, 64, 1024], P('group', 'lev', 'row'), parts along dimension 0
- modal_flux: float32 [6, 8, 64, 1024], P('group', None, 'row', 'lev'), parts along dimension 0
The draws below stay inside these ranges and needn't reach their ends.
There are 2 independent parts, one for each index of `group`. The reference program is written for one: setup_inputs(seed, part) draws one part's arguments, and reference() takes and returns one part's arrays. A program takes and returns all parts, laid end to end along the dimension named above; an argument that names none is the same for every part. Nothing has to cross between parts.
All inputs are finite; a program needn't handle non-finite values. No bound on the sum of `land_mask` on one device may be relied on, other than what follows from the above.
Results may differ from the reference program's by a relative error of at most 0.00092.
Values may be sent and summed in bfloat16 or wider, within the bound.
A program may use at most 192 MiB of HBM per device.

```python
import math
import jax
import jax.numpy as jnp
from jax import lax

L = 90
K = 8
NX = 1024
ITERS = 10
NY = 64


def plant(array, stream_key, least, top_value):
    longest = array.shape.index(max(array.shape))
    spots = []
    for shift in (0, 1):
        where = [jax.random.randint(jax.random.fold_in(stream_key, axis), (), 0, length) for axis, length in enumerate(array.shape)]
        where[longest] = (where[longest] + shift) % array.shape[longest]
        spots.append(tuple(where))
    return array.at[spots[0]].set(least).at[spots[1]].set(top_value)


def steps_of(stream_key, extent, split, low, largest):
    gain = 1.0
    for dim, blocks in split:
        steps = jax.random.uniform(jax.random.fold_in(jax.random.fold_in(stream_key, 6), dim), (blocks,), jnp.float32, low / len(split), largest / len(split))
        gain = gain * jnp.repeat(jnp.exp(steps), extent[dim] // blocks).reshape((-1,) + (1,) * (len(extent) - 1 - dim))
    return gain


def gaussian(own_key, dims, deviation, limit, shards=(), kind=jnp.bfloat16):
    entries = jax.random.normal(own_key, dims, jnp.float32) * deviation
    if len(shards) > 0:
        entries = steps_of(own_key, dims, shards, -0.22, 0.18) * entries
    return jnp.clip(entries, min=-limit, max=limit).astype(kind)


def setup_inputs(seed: int = 0, part: int = 0) -> dict:
    key_list = jax.random.split(jax.random.key(seed), 6)
    part_splits = jax.random.split(jax.random.fold_in(key_list[5], part), 6)
    return {
        "fields": gaussian(part_splits[0], (3, L, NY, NX), 1.0, 6.0, ((1, 2), (2, 8))),
        "vertical_modes": gaussian(key_list[1], (K, L, NY, NX), L ** -0.5, 0.625, ((1, 2), (2, 8))),
        "diffusivity": jnp.clip(jnp.exp(math.log(0.245) - 1.5892352 * jax.random.uniform(key_list[2], (NY, NX), jnp.float32) ** steps_of(key_list[2], (NY, NX), ((0, 8),), -0.2, 0.2)), 0.05, 0.245),
        "land_mask": plant((jax.random.randint(key_list[3], (NY, NX), 0, 10) < 9).astype(jnp.int32), jax.random.fold_in(key_list[3], 1), 0, 1),
        "wet_levels": plant(jax.random.randint(key_list[4], (NY, NX), 1, L + 1), jax.random.fold_in(key_list[4], 1), 1, L).astype(jnp.int32),
    }


def reference(fields, vertical_modes, diffusivity, land_mask, wet_levels):
    level_index = jnp.arange(L, dtype=jnp.int32)
    wet_cells = ((land_mask[None] == 1) & (level_index[:, None, None] < wet_levels[None])).astype(jnp.float32)
    east_weight = 0.5 * (diffusivity[:, :-1] + diffusivity[:, 1:])[None] * wet_cells[:, :, :-1] * wet_cells[:, :, 1:]
    north_weight = 0.5 * (diffusivity[:-1] + diffusivity[1:])[None] * wet_cells[:, :-1] * wet_cells[:, 1:]
    current = fields.astype(jnp.float32)
    for step_index in range(ITERS):
        east_flux = east_weight * (current[..., 1:] - current[..., :-1])
        north_flux = north_weight * (current[..., 1:, :] - current[..., :-1, :])
        east_side = jnp.pad(east_flux, ((0, 0), (0, 0), (0, 0), (0, 1))) - jnp.pad(east_flux, ((0, 0), (0, 0), (0, 0), (1, 0)))
        north_side = jnp.pad(north_flux, ((0, 0), (0, 0), (0, 1), (0, 0))) - jnp.pad(north_flux, ((0, 0), (0, 0), (1, 0), (0, 0)))
        current = current + east_side + north_side
    filtered = current.astype(jnp.bfloat16)
    modes_wide = vertical_modes.astype(jnp.float32)
    rounded_wide = filtered.astype(jnp.float32)
    amplitude = jnp.stack([jnp.einsum("klyx,lyx->kyx", modes_wide, rounded_wide[field_index], precision=lax.Precision.HIGHEST) for field_index in range(3)])
    modal_flux = jnp.stack([amplitude[0] * amplitude[2], amplitude[1] * amplitude[2], 0.5 * (amplitude[0] * amplitude[0] + amplitude[1] * amplitude[1])])
    return filtered, modal_flux
```

```python
import jax
import jax.numpy as jnp
from jax import lax
from jax.experimental import pallas as pl
from jax.experimental.pallas import tpu as pltpu
from jax.sharding import PartitionSpec as P

ITERS = 10
GROUP = 8


def shifted(value, axis, step):
    size = lax.axis_size(axis)
    pairs = [(i, i + step) for i in range(size) if 0 <= i + step < size]
    return lax.ppermute(value, axis, pairs)


def swapped(value, axis):
    size = lax.axis_size(axis)
    return lax.ppermute(value, axis, [(i, i ^ 1) for i in range(size)])


def pair_window(keep, other, odd):
    strip = keep.shape[0]
    lower = jnp.where(odd, other, keep)
    upper = jnp.where(odd, keep, other)
    rest = ITERS - strip
    before = shifted(jnp.concatenate([lower[strip - rest :], upper]), "row", 2)
    after = shifted(jnp.concatenate([lower, upper[:rest]]), "row", -2)
    return lower, upper, before, after


def smooth_kernel(info, stat, keep, other, before, after, own, back, cur, east, north):
    odd, level0 = info[0], info[1]
    strip, count = keep.shape[0], keep.shape[1]
    halo = before.shape[0]
    rows, width = cur.shape[1], cur.shape[3]
    level = (level0 + lax.broadcasted_iota(jnp.int32, (GROUP, width), 0)).astype(jnp.float32)
    mine = halo + strip * odd
    theirs = halo + strip * (1 - odd)

    @pl.loop(0, rows)
    def _(r):
        row = stat[r]
        east[r] = jnp.where(level < row[1:2], row[0:1], 0.0)
        north[r] = jnp.where(level < row[3:4], row[2:3], 0.0)

    def fill(source, start):
        @pl.loop(0, source.shape[0])
        def _(r):
            for f in range(count):
                cur[f, start + r] = source[r, f].astype(jnp.float32)

    fill(before, 0)
    fill(keep, mine)
    fill(other, theirs)
    fill(after, halo + 2 * strip)

    def one_row(f, r, here, south):
        above = cur[f, r + 1]
        north_flux = north[r] * (above - here)
        east_flux = east[r] * (pltpu.roll(here, width - 1, 1) - here)
        east_side = east_flux - pltpu.roll(east_flux, 1, 1)
        cur[f, r] = here + east_side + (north_flux - south)
        return above, north_flux

    @pl.loop(0, count)
    def _(f):
        @pl.loop(0, halo)
        def _(s):
            first = s + 1
            here = cur[f, first]
            south = north[s] * (here - cur[f, s])

            def two_rows(i, carry):
                r = first + 2 * i
                carry = one_row(f, r, *carry)
                return one_row(f, r + 1, *carry)

            lax.fori_loop(0, rows // 2 - 1 - s, two_rows, (here, south))

    @pl.loop(0, strip)
    def _(r):
        for f in range(count):
            own[r, f] = cur[f, mine + r].astype(own.dtype)
            back[r, f] = cur[f, theirs + r].astype(back.dtype)


def smooth(info, stat, keep, other, before, after):
    strip, count, _, width = keep.shape
    rows = 2 * strip + 2 * ITERS
    vmem = pl.BlockSpec(memory_space=pltpu.VMEM)
    steps = (rows - ITERS - 1) * ITERS * count * GROUP * width
    return pl.pallas_call(
        smooth_kernel,
        out_shape=[jax.ShapeDtypeStruct(keep.shape, keep.dtype)] * 2,
        in_specs=[pl.BlockSpec(memory_space=pltpu.SMEM)] + [vmem] * 5,
        out_specs=[vmem] * 2,
        scratch_shapes=[
            pltpu.VMEM((count, rows, GROUP, width), jnp.float32),
            pltpu.VMEM((rows, GROUP, width), jnp.float32),
            pltpu.VMEM((rows, GROUP, width), jnp.float32),
        ],
        compiler_params=pltpu.CompilerParams(vmem_limit_bytes=32 << 20),
        cost_estimate=pl.CostEstimate(
            flops=10 * steps, bytes_accessed=8 << 20, transcendentals=0
        ),
        name="smooth",
    )(info, stat, keep, other, before, after)


def project_kernel(fields, modes, out):
    count, levels, rows, width = fields.shape
    kinds = modes.shape[0]
    for start in range(0, width, 128):
        cols = pl.ds(start, 128)

        def add(l, sums):
            f = [fields[i, l, :, cols].astype(jnp.float32) for i in range(count)]
            new = []
            for k in range(kinds):
                m = modes[k, l, :, cols].astype(jnp.float32)
                new += [sums[k * count + i] + m * f[i] for i in range(count)]
            return tuple(new)

        zero = jnp.zeros((rows, 128), jnp.float32)
        sums = lax.fori_loop(0, levels, add, (zero,) * (count * kinds))
        for k in range(kinds):
            for i in range(count):
                out[0, i, k, :, cols] = sums[k * count + i]


def project(fields, modes, parts):
    count, levels, rows, width = fields.shape
    kinds = modes.shape[0]
    tile = 256
    per = width // parts // tile
    return pl.pallas_call(
        project_kernel,
        grid=(parts * per,),
        out_shape=jax.ShapeDtypeStruct((parts, count, kinds, rows, width // parts), jnp.float32),
        in_specs=[
            pl.BlockSpec((count, levels, rows, tile), lambda j: (0, 0, 0, j)),
            pl.BlockSpec((kinds, levels, rows, tile), lambda j: (0, 0, 0, j)),
        ],
        out_specs=pl.BlockSpec(
            (1, count, kinds, rows, tile), lambda j: (j // per, 0, 0, 0, j % per)
        ),
        compiler_params=pltpu.CompilerParams(vmem_limit_bytes=32 << 20),
        cost_estimate=pl.CostEstimate(
            flops=2 * count * kinds * levels * rows * width,
            bytes_accessed=2 * (count + kinds) * levels * rows * width,
            transcendentals=0,
        ),
        name="project",
    )(fields, modes)


def per_device(fields, vertical_modes, diffusivity, land_mask, wet_levels):
    levels = fields.shape[1]
    strip = fields.shape[2]
    odd = lax.axis_index("row") % 2 == 1
    groups = -(-(levels + 1) // 2 // GROUP)
    span = groups * GROUP
    top = levels - span

    depth = (land_mask * wet_levels).astype(jnp.float32)
    statics = jnp.stack([diffusivity, depth], axis=1)
    lower, upper, before, after = pair_window(statics, swapped(statics, "row"), odd)
    whole = jnp.concatenate([before, lower, upper, after])
    diff, deep = whole[:, 0], whole[:, 1]
    east = 0.5 * (diff + jnp.roll(diff, -1, 1))
    is_last = jnp.arange(diff.shape[1]) == diff.shape[1] - 1
    east_deep = jnp.where(is_last[None], 0.0, jnp.minimum(deep, jnp.roll(deep, -1, 1)))
    north = 0.5 * (diff + jnp.roll(diff, -1, 0))
    north_deep = jnp.minimum(deep, jnp.roll(deep, -1, 0))
    stat = jnp.stack([east, east_deep, north, north_deep], axis=1)

    by_row = jnp.transpose(fields, (2, 0, 1, 3))
    start = lax.axis_index("lev") * levels + jnp.where(odd, top, 0)
    kept, returned = [], []
    last = None
    for g in range(groups):
        low = by_row[:, :, g * GROUP : (g + 1) * GROUP]
        high = by_row[:, :, top + g * GROUP : top + (g + 1) * GROUP]
        keep = jnp.where(odd, high, low)
        give = jnp.where(odd, low, high)
        if last is not None:
            give, last = lax.optimization_barrier((give, last))
        other = last = swapped(give, "row")
        _, _, before, after = pair_window(keep, other, odd)
        info = jnp.stack([odd.astype(jnp.int32), (start + g * GROUP).astype(jnp.int32)])
        own, back = smooth(info, stat, keep, other, before, after)
        kept.append(own)
        returned.append(swapped(back, "row"))
    kept, returned = jnp.concatenate(kept, 2), jnp.concatenate(returned, 2)
    low = jnp.where(odd, returned, kept)
    high = jnp.where(odd, kept, returned)
    filtered = jnp.concatenate([low, high[:, :, span - top :]], axis=2)
    filtered = jnp.transpose(filtered, (1, 2, 0, 3))

    parts = lax.axis_size("lev")
    terms = project(filtered, vertical_modes, parts)
    here = lax.axis_index("lev")
    amplitude = lax.dynamic_index_in_dim(terms, here, 0, keepdims=False)
    for step in range(1, parts):
        away = lax.dynamic_index_in_dim(terms, (here + step) % parts, 0, keepdims=False)
        ring = [(i, (i + step) % parts) for i in range(parts)]
        amplitude = amplitude + lax.ppermute(away, "lev", ring)
    modal_flux = jnp.stack(
        [
            amplitude[0] * amplitude[2],
            amplitude[1] * amplitude[2],
            0.5 * (amplitude[0] * amplitude[0] + amplitude[1] * amplitude[1]),
        ]
    )
    return (filtered, modal_flux)


def solution(mesh):
    placed = (
        P("group", "lev", "row", None),
        P(None, "lev", "row", None),
        P("row", None),
        P("row", None),
        P("row", None),
    )
    return jax.shard_map(
        per_device,
        mesh=mesh,
        in_specs=placed,
        out_specs=(P("group", "lev", "row", None), P("group", None, "row", "lev")),
        check_vma=False,
    )
```

```python
import jax
import jax.numpy as jnp
from jax import lax
from jax.experimental import pallas as pl
from jax.experimental.pallas import tpu as pltpu
from jax.sharding import PartitionSpec as P

ITERS = 10
GROUP = 8


def shifted(value, axis, step):
    size = lax.axis_size(axis)
    pairs = [(i, i + step) for i in range(size) if 0 <= i + step < size]
    return lax.ppermute(value, axis, pairs)


def swapped(value, axis):
    size = lax.axis_size(axis)
    return lax.ppermute(value, axis, [(i, i ^ 1) for i in range(size)])


def pair_window(keep, other, odd):
    strip = keep.shape[0]
    lower = jnp.where(odd, other, keep)
    upper = jnp.where(odd, keep, other)
    rest = ITERS - strip
    before = shifted(jnp.concatenate([lower[strip - rest :], upper]), "row", 2)
    after = shifted(jnp.concatenate([lower, upper[:rest]]), "row", -2)
    return lower, upper, before, after


def smooth_kernel(info, stat, keep, other, before, after, own, back, cur, nxt, east, west, north):
    odd, level0 = info[0], info[1]
    strip, count = keep.shape[0], keep.shape[1]
    halo = before.shape[0]
    rows, width = cur.shape[1], cur.shape[3]
    level = (level0 + lax.broadcasted_iota(jnp.int32, (GROUP, width), 0)).astype(jnp.float32)
    mine = halo + strip * odd
    theirs = halo + strip * (1 - odd)

    @pl.loop(0, rows)
    def _(r):
        row = stat[r]
        east[r] = jnp.where(level < row[1:2], row[0:1], 0.0)
        west[r] = pltpu.roll(east[r], 1, 1)
        north[r] = jnp.where(level < row[3:4], row[2:3], 0.0)

    def fill(source, start):
        @pl.loop(0, source.shape[0])
        def _(r):
            for f in range(count):
                cur[f, start + r] = source[r, f].astype(jnp.float32)

    fill(before, 0)
    fill(keep, mine)
    fill(other, theirs)
    fill(after, halo + 2 * strip)

    def one_step(source, target, s):
        @pl.loop(0, rows // 2 - 1 - s)
        def _(i):
            r = s + 1 + 2 * i
            for f in range(count):
                held = [source[f, r + d] for d in range(-1, 3)]
                side = [north[r - 1 + d] * (held[d + 1] - held[d]) for d in range(3)]
                for d in range(2):
                    here = held[d + 1]
                    east_flux = east[r + d] * (pltpu.roll(here, width - 1, 1) - here)
                    west_flux = west[r + d] * (here - pltpu.roll(here, 1, 1))
                    target[f, r + d] = here + (east_flux - west_flux) + (side[d + 1] - side[d])

    @pl.loop(0, halo // 2)
    def _(j):
        one_step(cur, nxt, 2 * j)
        one_step(nxt, cur, 2 * j + 1)

    @pl.loop(0, strip)
    def _(r):
        for f in range(count):
            own[r, f] = cur[f, mine + r].astype(own.dtype)
            back[r, f] = cur[f, theirs + r].astype(back.dtype)


def smooth(info, stat, keep, other, before, after):
    strip, count, _, width = keep.shape
    rows = 2 * strip + 2 * ITERS
    vmem = pl.BlockSpec(memory_space=pltpu.VMEM)
    steps = (rows - ITERS - 1) * ITERS * count * GROUP * width
    return pl.pallas_call(
        smooth_kernel,
        out_shape=[jax.ShapeDtypeStruct(keep.shape, keep.dtype)] * 2,
        in_specs=[pl.BlockSpec(memory_space=pltpu.SMEM)] + [vmem] * 5,
        out_specs=[vmem] * 2,
        scratch_shapes=[
            pltpu.VMEM((count, rows, GROUP, width), jnp.float32),
            pltpu.VMEM((count, rows, GROUP, width), jnp.float32),
            pltpu.VMEM((rows, GROUP, width), jnp.float32),
            pltpu.VMEM((rows, GROUP, width), jnp.float32),
            pltpu.VMEM((rows, GROUP, width), jnp.float32),
        ],
        compiler_params=pltpu.CompilerParams(vmem_limit_bytes=32 << 20),
        cost_estimate=pl.CostEstimate(
            flops=10 * steps, bytes_accessed=8 << 20, transcendentals=0
        ),
        name="smooth",
    )(info, stat, keep, other, before, after)


def project_kernel(fields, modes, out):
    count, levels, rows, width = fields.shape
    kinds = modes.shape[0]
    for start in range(0, width, 128):
        cols = pl.ds(start, 128)

        def add(l, sums):
            f = [fields[i, l, :, cols].astype(jnp.float32) for i in range(count)]
            new = []
            for k in range(kinds):
                m = modes[k, l, :, cols].astype(jnp.float32)
                new += [sums[k * count + i] + m * f[i] for i in range(count)]
            return tuple(new)

        zero = jnp.zeros((rows, 128), jnp.float32)
        sums = lax.fori_loop(0, levels, add, (zero,) * (count * kinds))
        for k in range(kinds):
            for i in range(count):
                out[0, i, k, :, cols] = sums[k * count + i]


def project(fields, modes, parts):
    count, levels, rows, width = fields.shape
    kinds = modes.shape[0]
    tile = 256
    per = width // parts // tile
    return pl.pallas_call(
        project_kernel,
        grid=(parts * per,),
        out_shape=jax.ShapeDtypeStruct((parts, count, kinds, rows, width // parts), jnp.float32),
        in_specs=[
            pl.BlockSpec((count, levels, rows, tile), lambda j: (0, 0, 0, j)),
            pl.BlockSpec((kinds, levels, rows, tile), lambda j: (0, 0, 0, j)),
        ],
        out_specs=pl.BlockSpec(
            (1, count, kinds, rows, tile), lambda j: (j // per, 0, 0, 0, j % per)
        ),
        compiler_params=pltpu.CompilerParams(vmem_limit_bytes=32 << 20),
        cost_estimate=pl.CostEstimate(
            flops=2 * count * kinds * levels * rows * width,
            bytes_accessed=2 * (count + kinds) * levels * rows * width,
            transcendentals=0,
        ),
        name="project",
    )(fields, modes)


def per_device(fields, vertical_modes, diffusivity, land_mask, wet_levels):
    levels = fields.shape[1]
    strip = fields.shape[2]
    odd = lax.axis_index("row") % 2 == 1
    groups = -(-(levels + 1) // 2 // GROUP)
    span = groups * GROUP
    top = levels - span

    depth = (land_mask * wet_levels).astype(jnp.float32)
    statics = jnp.stack([diffusivity, depth], axis=1)
    lower, upper, before, after = pair_window(statics, swapped(statics, "row"), odd)
    whole = jnp.concatenate([before, lower, upper, after])
    diff, deep = whole[:, 0], whole[:, 1]
    east = 0.5 * (diff + jnp.roll(diff, -1, 1))
    is_last = jnp.arange(diff.shape[1]) == diff.shape[1] - 1
    east_deep = jnp.where(is_last[None], 0.0, jnp.minimum(deep, jnp.roll(deep, -1, 1)))
    north = 0.5 * (diff + jnp.roll(diff, -1, 0))
    north_deep = jnp.minimum(deep, jnp.roll(deep, -1, 0))
    stat = jnp.stack([east, east_deep, north, north_deep], axis=1)

    by_row = jnp.transpose(fields, (2, 0, 1, 3))
    start = lax.axis_index("lev") * levels + jnp.where(odd, top, 0)
    kept, returned = [], []
    for g in range(groups):
        low = by_row[:, :, g * GROUP : (g + 1) * GROUP]
        high = by_row[:, :, top + g * GROUP : top + (g + 1) * GROUP]
        keep = jnp.where(odd, high, low)
        give = jnp.where(odd, low, high)
        other = swapped(give, "row")
        _, _, before, after = pair_window(keep, other, odd)
        info = jnp.stack([odd.astype(jnp.int32), (start + g * GROUP).astype(jnp.int32)])
        own, back = smooth(info, stat, keep, other, before, after)
        kept.append(own)
        returned.append(swapped(back, "row"))
    kept, returned = jnp.concatenate(kept, 2), jnp.concatenate(returned, 2)
    low = jnp.where(odd, returned, kept)
    high = jnp.where(odd, kept, returned)
    filtered = jnp.concatenate([low, high[:, :, span - top :]], axis=2)
    filtered = jnp.transpose(filtered, (1, 2, 0, 3))

    parts = lax.axis_size("lev")
    terms = project(filtered, vertical_modes, parts)
    here = lax.axis_index("lev")
    amplitude = lax.dynamic_index_in_dim(terms, here, 0, keepdims=False)
    for step in range(1, parts):
        away = lax.dynamic_index_in_dim(terms, (here + step) % parts, 0, keepdims=False)
        ring = [(i, (i + step) % parts) for i in range(parts)]
        amplitude = amplitude + lax.ppermute(away, "lev", ring)
    modal_flux = jnp.stack(
        [
            amplitude[0] * amplitude[2],
            amplitude[1] * amplitude[2],
            0.5 * (amplitude[0] * amplitude[0] + amplitude[1] * amplitude[1]),
        ]
    )
    return (filtered, modal_flux)


def solution(mesh):
    placed = (
        P("group", "lev", "row", None),
        P(None, "lev", "row", None),
        P("row", None),
        P("row", None),
        P("row", None),
    )
    return jax.shard_map(
        per_device,
        mesh=mesh,
        in_specs=placed,
        out_specs=(P("group", "lev", "row", None), P("group", None, "row", "lev")),
        check_vma=False,
    )
```
